512 devices in a mesh: lists: 64 (over x, y, core), qb: 8 (over z).
Axes of the slice: x: 4, y: 8, z: 8, core: 2. Of those that a mesh axis runs over, the one named last changes fastest.
Arguments:
- queries: float32 [16384, 128], P(('lists', 'qb')), may hold values from -28 to 28
- reader_logits: float32 [16384, 16], P(('lists', 'qb')), may hold values from -8 to 8
- probe_shards: int32 [16384, 16], P(('lists', 'qb')), may hold values from 0 to 63, all different within a row; in each aligned block of 32 rows (0 to 31, 32 to 63, ...) at most 16 rows name the same one
- probe_within: int32 [16384, 16], P(('lists', 'qb')), may hold values from 0 to 7
- passages: float32 [49152, 128], P('lists'), may hold values from -6 to 6
- list_sizes: int32 [64, 8], P('lists'), may hold values from 1 to 192, 768 in all within a row
Outputs:
- query_grad: float32 [16384, 128], P(('lists', 'qb'))
- passage_grad: float32 [49152, 128], P(('lists', 'qb'))
- query_loss: float32 [16384], P(('lists', 'qb'))
The draws below stay inside these ranges and needn't reach their ends.
Inputs may be any that keep to these rules, and one draw needn't show every extreme that they name: `probe_shards`: each row names 16 different values. Among the rows of one device no value is named by more than 16 rows, a bound that some block reaches. `list_sizes`: each row sums to 768, and its largest entry is 192.
All inputs are finite; a program needn't handle non-finite values.
Results may differ from the reference program's by a relative error of at most 0.0003.
Values sent between devices are 32-bit elements; how exact they have to be, the bound alone decides.
A program may use at most 64 MiB of HBM per device.

```python
import math
import jax
import jax.numpy as jnp
import numpy as np
from jax import lax

EMB = 128
PROBES = 16
QUERIES_DEV = 32
PASS_DEV = 768
LISTS_DEV = 8
LMOST = 192
CAP = 16
QUERIES = 16384
PASSAGES = 49152
N_LISTS = 64


def draw_queries(key, part):
    key = jax.random.fold_in(key, 11)
    rows_out = jnp.clip(jax.random.normal(key, (QUERIES, EMB), jnp.float32), -6.0, 6.0)
    return rows_out.astype(jnp.float32)


def draw_passages(key, part):
    key = jax.random.fold_in(key, 23)
    rows_out = jnp.clip(jax.random.normal(key, (PASSAGES, EMB), jnp.float32), -6.0, 6.0)
    return rows_out.astype(jnp.float32)


def set_ends(result, rng, smallest, largest):
    extent = result.shape
    spot = [jax.random.randint(jax.random.fold_in(rng, axis), (), 0, extent[axis]) for axis in range(len(extent))]
    result = result.at[tuple(spot)].set(smallest)
    longest = extent.index(max(extent))
    spot[longest] = (spot[longest] + 1) % extent[longest]
    return result.at[tuple(spot)].set(largest)


def steps_of(stream_key, extent, cuts, low, top_value):
    gain, own = 1.0, jax.random.fold_in(stream_key, 6)
    for dim, blocks in cuts:
        steps = jnp.exp(jax.random.uniform(jax.random.fold_in(own, dim), (blocks,), jnp.float32, low / len(cuts), top_value / len(cuts)))
        gain = gain * jnp.repeat(steps, extent[dim] // blocks).reshape([-1 if axis == dim else 1 for axis in range(len(extent))])
    return gain


def profile(amount, total, bound, slope):
    weights = [(1 << 20) // math.isqrt(rank ** slope) + 1 for rank in range(2, amount + 1)]
    rest, given = total - bound - (amount - 1), [1] * (amount - 1)
    while rest > 0:
        candidates = [i for i in range(amount - 1) if given[i] < bound]
        whole, left = sum([weights[i] for i in candidates]), rest
        for i in candidates:
            more = min(bound - given[i], max(1, left * weights[i] // whole), rest)
            given[i] = given[i] + more
            rest = rest - more
    return np.array([bound] + given)


def uneven(key, number_of, total, reach, skew):
    if number_of == 2:
        one = jax.random.randint(key, (), max(1, total - reach), min(reach, total - 1) + 1)
        return jnp.stack([one, total - one])
    tallies = jnp.asarray(profile(number_of, total, reach, skew), jnp.int32)
    couples = (number_of - 1) // 2
    donor, receiver = tallies[1:1 + 2 * couples:2], tallies[2:2 + 2 * couples:2]
    room = jnp.minimum(donor - 1, reach - receiver)
    moved = jax.random.randint(jax.random.fold_in(key, 1), (couples,), 0, 1 << 20) % (room + 1)
    tallies = tallies.at[1:1 + 2 * couples:2].set(donor - moved).at[2:2 + 2 * couples:2].set(receiver + moved)
    return tallies[jax.random.permutation(jax.random.fold_in(key, 2), number_of)]


def routed_block(key, own, number, rows, count, top, most, skew):
    ranking = jax.random.permutation(key, count)
    packed, usual = portions_of(count, rows * top, most, skew, True), portions_of(count, rows * top, most, skew, False)
    places = jnp.arange(count)

    def named(lengths, rotation):
        used = int((lengths > 0).sum())
        fixed = max(1, used // 4)
        shifted = fixed + (places - fixed + rotation * (used - fixed)) % max(1, count - fixed)
        return jnp.zeros((count,), jnp.int32).at[ranking[jnp.where(places < fixed, places, shifted)]].set(jnp.asarray(lengths, jnp.int32))

    lengths = jnp.where(number % 4 == 0, named(packed, number // 4), named(usual, number - number // 4 - 1))
    mixed = jax.random.permutation(jax.random.fold_in(own, 3), count)
    source_of, taker = mixed[0:count // 2 * 2:2], mixed[1:count // 2 * 2:2]
    slack = jnp.minimum(lengths[source_of] - 1, most - lengths[taker]) // 2
    slack = jnp.where((source_of == ranking[0]) | (taker == ranking[0]) | (lengths[taker] == 0), 0, jnp.maximum(slack, 0))
    shifted = jax.random.randint(jax.random.fold_in(own, 4), (count // 2,), 0, 1 << 20) % (slack + 1)
    lengths = lengths.at[source_of].add(-shifted).at[taker].add(shifted)
    items = jnp.searchsorted(jnp.cumsum(lengths), jnp.arange(rows * top), side="right").astype(jnp.int32)
    table = items.reshape(top, rows).T
    table = table[jax.random.permutation(jax.random.fold_in(own, 1), rows)]
    rotation = jax.random.randint(jax.random.fold_in(own, 2), (rows, 1), 0, top)
    return jnp.take_along_axis(table, (jnp.arange(top)[None, :] + rotation) % top, axis=1)


def portions_of(amount, total, limit, skew, full):
    loads = [(1 << 20) // math.isqrt(standing ** skew) + 1 for standing in range(1, amount + 1)]
    largest = limit if full else min(limit, max(-(-total // amount), total * loads[0] // sum(loads)))
    least = 1 if total - largest >= amount - 1 else 0
    holding, surplus = [largest] + [least] * (amount - 1), total - largest - least * (amount - 1)
    while surplus > 0:
        movable = [i for i in range(1, amount) if holding[i] < largest] or [i for i in range(1, amount) if holding[i] < limit]
        pool, remaining = sum([loads[i] for i in movable]), surplus
        for i in movable:
            extra = min(limit - holding[i], max(1, remaining * loads[i] // pool), surplus)
            holding[i] = holding[i] + extra
            surplus = surplus - extra
    return np.array(holding)


def scatter_about(stream_key, shape, spread, reach, cuts=(), kind=jnp.bfloat16):
    loudness = steps_of(stream_key, shape, cuts, -0.22, 0.18) if cuts else 1.0
    array = jax.random.normal(stream_key, shape, jnp.float32) * spread * loudness
    return jnp.minimum(jnp.maximum(array, -reach), reach).astype(kind)


def setup_inputs(seed: int = 0) -> dict:
    streams_of = jax.random.split(jax.random.key(seed), 7)
    queries = draw_queries(jax.random.fold_in(streams_of[6], 71), 0)
    reader_logits = scatter_about(streams_of[1], (QUERIES, PROBES), 2.0, 8.0, ((0, 512),), jnp.float32)
    probe_shards_keys = jax.random.split(jax.random.fold_in(streams_of[2], 1), QUERIES // QUERIES_DEV)
    probe_shards_turns = jax.random.permutation(jax.random.fold_in(streams_of[2], 3), QUERIES // QUERIES_DEV)
    probe_shards = jax.vmap(lambda own, number: routed_block(jax.random.fold_in(streams_of[2], 2), own, number, QUERIES_DEV, N_LISTS, PROBES, CAP, 2))(probe_shards_keys, probe_shards_turns).reshape((QUERIES, PROBES))
    probe_within = set_ends(jax.random.randint(streams_of[3], (QUERIES, PROBES), 0, LISTS_DEV), jax.random.fold_in(streams_of[3], 1), 0, LISTS_DEV - 1).astype(jnp.int32)
    passages = draw_passages(jax.random.fold_in(streams_of[6], 71), 0)
    list_sizes = jax.vmap(lambda own: uneven(own, LISTS_DEV, PASS_DEV, LMOST, 2))(jax.random.split(streams_of[5], N_LISTS)).reshape((N_LISTS, LISTS_DEV)).astype(jnp.int32)
    return {"queries": queries, "reader_logits": reader_logits, "probe_shards": probe_shards, "probe_within": probe_within, "passages": passages, "list_sizes": list_sizes}


def reference(queries, reader_logits, probe_shards, probe_within, passages, list_sizes):
    score_scale = 1.0 / math.sqrt(EMB)
    sizes_int = list_sizes.astype(jnp.int32)
    flat_sizes = sizes_int.reshape(-1)
    inner_start = jnp.cumsum(sizes_int, axis=1) - sizes_int
    shard_base = (jnp.arange(N_LISTS, dtype=jnp.int32) * PASS_DEV)[:, None]
    list_start = (inner_start + shard_base).reshape(-1).astype(jnp.int32)
    column = jnp.arange(LMOST, dtype=jnp.int32)
    member = column[None, :] < flat_sizes[:, None]
    table = jnp.where(member, list_start[:, None] + column[None, :], 0).astype(jnp.int32)
    list_ids = (probe_shards * LISTS_DEV + probe_within).astype(jnp.int32)
    step_count = QUERIES // QUERIES_DEV
    inputs_all = (queries.reshape(step_count, QUERIES_DEV, EMB), reader_logits.reshape(step_count, QUERIES_DEV, PROBES), list_ids.reshape(step_count, QUERIES_DEV, PROBES))

    def one_block(passage_acc, inputs):
        query_rows, logits, probe_lists = inputs
        rows_index = table[probe_lists]
        usable = member[probe_lists]
        gathered = passages[rows_index]
        scores = score_scale * jnp.einsum('bd,bkjd->bkj', query_rows, gathered, precision=lax.Precision.HIGHEST)
        row_top = lax.optimization_barrier(jnp.max(jnp.where(usable, scores, -jnp.inf), axis=2))
        expo_terms = jnp.where(usable, jnp.exp(scores - row_top[..., None]), 0.0)
        probe_norm = lax.optimization_barrier(jnp.sum(expo_terms, axis=2))
        query_peak = lax.optimization_barrier(jnp.max(row_top, axis=1))
        probe_mass = probe_norm * jnp.exp(row_top - query_peak[:, None])
        mass_total = lax.optimization_barrier(jnp.sum(probe_mass, axis=1))
        probe_share = probe_mass / mass_total[:, None]
        log_share = jnp.log(probe_norm) + (row_top - query_peak[:, None]) - jnp.log(mass_total)[:, None]
        log_target = jax.nn.log_softmax(logits, axis=1)
        reader_share = jnp.exp(log_target)
        query_loss = lax.optimization_barrier(jnp.sum(reader_share * (log_target - log_share), axis=1))
        coefficient = (probe_share - reader_share) / probe_norm
        weight = expo_terms * coefficient[..., None]
        query_grad = score_scale * jnp.einsum('bkj,bkjd->bd', weight, gathered, precision=lax.Precision.HIGHEST)
        update = score_scale * weight[..., None] * query_rows[:, None, None, :]
        passage_acc = passage_acc.at[rows_index].add(update)
        return (passage_acc, (query_grad, query_loss))
    start_acc = jnp.zeros((PASSAGES, EMB), jnp.float32)
    passage_grad, outputs = lax.scan(one_block, start_acc, inputs_all)
    query_grad = outputs[0].reshape(QUERIES, EMB)
    query_loss = outputs[1].reshape(QUERIES)
    return (query_grad, passage_grad, query_loss)
```

```python
import functools
import math

import jax
import jax.numpy as jnp
from jax import lax
from jax.experimental import pallas as pl
from jax.experimental.pallas import tpu as pltpu
from jax.sharding import PartitionSpec as P

MESH = pl.DeviceIdType.MESH
F32, BF16, I32 = jnp.float32, jnp.bfloat16, jnp.int32
LOW = -1e30
GROUP = 8


def split3(x):
    hi = x.astype(BF16)
    rest = x - hi.astype(F32)
    mid = rest.astype(BF16)
    low = (rest - mid.astype(F32)).astype(BF16)
    return hi, mid, low


def split2(x):
    hi = x.astype(BF16)
    return hi, (x - hi.astype(F32)).astype(BF16)


def mm(a, b):
    return jnp.dot(a, b, preferred_element_type=F32)


def mm_nt(a, b):
    return lax.dot_general(a, b, (((1,), (1,)), ((), ())), preferred_element_type=F32)


def mm_tn(a, b):
    return lax.dot_general(a, b, (((0,), (0,)), ((), ())), preferred_element_type=F32)


def kernel(
    shards,
    groups,
    cap,
    q_hbm,
    lg_hbm,
    ps_hbm,
    pw_hbm,
    p_hbm,
    ls_hbm,
    qg_ref,
    pg_ref,
    loss_ref,
    q_v,
    lg_v,
    ps_v,
    pw_v,
    p_v,
    ls_v,
    meta_s,
    meta_r,
    rows_s,
    rows_r,
    stat_s,
    stat_r,
    coef_s,
    coef_r,
    u_s,
    u_r,
    z_s,
    z_r,
    expand,
    disp,
    logt,
    acoef,
    pcat,
    ptr,
    owner,
    eh,
    el,
    rch,
    rcm,
    in_sem,
    meta_ss,
    meta_rs,
    rows_ss,
    rows_rs,
    stat_ss,
    stat_rs,
    coef_ss,
    coef_rs,
    u_ss,
    u_rs,
    z_ss,
    z_rs,
):
    per_dev, emb = q_v.shape
    probes = ps_v.shape[1]
    pass_dev = p_v.shape[0]
    part = pass_dev // groups
    chunks = shards // GROUP
    width = GROUP * cap
    slots = shards * cap
    scale = 1.0 / math.sqrt(emb)
    me = lax.axis_index("lists")
    qb = lax.axis_index("qb")

    def peer(j):
        return {"lists": lax.rem(me + j, shards)}

    def source(j):
        return {"lists": lax.rem(me - j + shards, shards)}

    def to(src, dst, ss, rs, device):
        return pltpu.make_async_remote_copy(
            src_ref=src, dst_ref=dst, send_sem=ss, recv_sem=rs, device_id=device, device_id_type=MESH
        )

    order = [
        (groups // 2 + ((i % 2) * 2 - 1) * ((i + 1) // 2)) % groups for i in range(groups)
    ]
    small = [(q_hbm, q_v), (ps_hbm, ps_v), (pw_hbm, pw_v), (lg_hbm, lg_v), (ls_hbm, ls_v)]
    loads = [pltpu.make_async_copy(a, b, in_sem.at[i]) for i, (a, b) in enumerate(small)]
    for i, d in enumerate(order):
        start = pl.multiple_of(lax.rem(qb + d, groups) * part, part)
        loads.append(
            pltpu.make_async_copy(
                p_hbm.at[pl.ds(start, part)], p_v.at[pl.ds(i * part, part)], in_sem.at[len(small) + i]
            )
        )
    for load in loads:
        load.start()

    barrier = pltpu.get_barrier_semaphore()

    def greet(j, carry):
        pl.semaphore_signal(barrier, inc=1, device_id=peer(j), device_id_type=MESH)
        return carry

    lax.fori_loop(1, shards, greet, 0)
    for d in range(1, groups):
        pl.semaphore_signal(
            barrier, inc=1, device_id={"qb": lax.rem(qb + d, groups)}, device_id_type=MESH
        )

    expand[...] = (
        lax.broadcasted_iota(I32, (shards, slots), 1) // cap
        == lax.broadcasted_iota(I32, (shards, slots), 0)
    ).astype(BF16)
    place = (lax.rem(lax.broadcasted_iota(I32, (per_dev, slots), 1), cap) + 1).astype(F32)
    tri = (
        lax.broadcasted_iota(I32, (per_dev, per_dev), 1)
        <= lax.broadcasted_iota(I32, (per_dev, per_dev), 0)
    ).astype(BF16)
    shard_lane = lax.broadcasted_iota(I32, (per_dev, shards), 1)
    for load in loads[:3]:
        load.wait()
    ps = ps_v[...]
    rel = jnp.where(ps >= me, ps - me, ps - me + shards)
    within = pw_v[...]
    w1 = jnp.zeros((per_dev, shards), F32)
    for k in range(probes):
        w1 = jnp.where(rel[:, k : k + 1] == shard_lane, (within[:, k : k + 1] + 1).astype(F32), w1)
    hot = w1 > 0.0
    rank = mm(tri, hot.astype(BF16))
    slot1 = jnp.where(hot, rank, 0.0)
    both = mm(jnp.concatenate([slot1, w1], axis=0).astype(BF16), expand[...])
    mask = both[:per_dev] == place
    disp[...] = mask.astype(F32)
    ids = jnp.sum(jnp.where(mask, both[per_dev:], 0.0), axis=0, keepdims=True)
    for c in range(chunks):
        meta_s[c] = ids[:, c * width : (c + 1) * width]
    q_scaled = q_v[...] * scale
    q3 = jnp.concatenate(split3(q_scaled), axis=0)
    for c in range(chunks):
        d1 = disp[:, c * width : (c + 1) * width].astype(BF16)
        block = mm_tn(jnp.concatenate([d1, d1, d1], axis=0), q3)
        rows_s[pl.ds(c * GROUP, GROUP)] = block.reshape(GROUP, cap, emb)

    pl.semaphore_wait(barrier, shards - 1 + groups - 1)

    def send_meta(j, carry):
        c = j // GROUP
        to(meta_s.at[c], meta_r.at[j], meta_ss, meta_rs.at[c], peer(j)).start()
        return carry

    def send_rows(j, carry):
        c = j // GROUP
        to(rows_s.at[j], rows_r.at[j], rows_ss, rows_rs.at[c], peer(j)).start()
        return carry

    def send_both(j, carry):
        return send_rows(j, send_meta(j, carry))

    lax.fori_loop(1, shards, send_both, 0)
    meta_r[0] = meta_s[0]
    rows_r[0] = rows_s[0]

    for load in loads[3:]:
        load.wait()
    p = p_v[...]
    ph, pm, plow = split3(p)
    pcat[...] = jnp.concatenate([ph, pm, ph, plow, ph, pm], axis=1)
    pth, ptm = split2(p.T)
    ptr[:, :pass_dev] = pth
    ptr[:, pass_dev:] = ptm
    end = jnp.zeros((1, 1), I32)
    for i, d in enumerate(order):
        first = lax.rem(qb + d, groups) * part
        number = lax.broadcasted_iota(I32, (part, width), 0) + first
        end = jnp.zeros((1, 1), I32)
        own = jnp.ones((part, width), F32)
        for g in range(ls_v.shape[1]):
            end = end + ls_v[:, g : g + 1]
            own = own + jnp.where(number >= end, 1.0, 0.0)
        owner[i * part : (i + 1) * part, :] = own

    lg = lg_v[...]
    lg = lg - jnp.max(lg, axis=1, keepdims=True)
    lt = lg - jnp.log(jnp.sum(jnp.exp(lg), axis=1, keepdims=True))
    lt_shard = jnp.zeros((per_dev, shards), F32)
    for k in range(probes):
        lt_shard = jnp.where(rel[:, k : k + 1] == shard_lane, lt[:, k : k + 1], lt_shard)
    lt3 = mm(jnp.concatenate(split3(lt_shard), axis=0), expand[...])
    logt[...] = lt3[:per_dev] + lt3[per_dev : 2 * per_dev] + lt3[2 * per_dev :]

    lane = lax.broadcasted_iota(I32, (1, width), 1) // cap

    def gather_row(ref, c, row):
        out = jnp.zeros((1, width), F32)
        for jj in range(GROUP):
            out = jnp.where(lane == jj, ref[c * GROUP + jj, row : row + 1, :], out)
        return out

    def wait_chunk(ref, sems, c):
        @pl.when(c == 0)
        def _():
            view = ref.at[pl.ds(1, GROUP - 1)]
            to(view, view, rows_ss, sems.at[0], peer(1)).wait_recv()

        @pl.when(c > 0)
        def _():
            view = ref.at[pl.ds(c * GROUP, GROUP)]
            to(view, view, rows_ss, sems.at[c], peer(1)).wait_recv()

    def forward(c, carry):
        wait_chunk(meta_r, meta_rs, c)
        ident = gather_row(meta_r, c, 0)
        wait_chunk(rows_r, rows_rs, c)
        rows = rows_r[pl.ds(c * GROUP, GROUP)].reshape(width, emb)
        rh, rm, rl = split3(rows)
        score = mm_nt(pcat[...], jnp.concatenate([rh, rh, rm, rh, rl, rm], axis=1))
        score = jnp.where(owner[...] == ident, score, LOW)
        top = jnp.max(score, axis=0, keepdims=True)
        expo = jnp.exp(score - top)
        norm = jnp.sum(expo, axis=0, keepdims=True)
        stat_s[c, 0:1, :] = top
        stat_s[c, 1:2, :] = norm

        def send_stat(jj, carry):
            j = c * GROUP + jj
            to(stat_s.at[c], stat_r.at[j], stat_ss, stat_rs, source(j)).start()
            return carry

        lax.fori_loop(jnp.where(c == 0, 1, 0), GROUP, send_stat, 0)
        hi, lo = split2(expo)
        at = pl.ds(pl.multiple_of(c * width, width), width)
        eh[:, at] = hi
        el[:, at] = lo
        return carry

    lax.fori_loop(0, chunks, forward, 0)
    stat_r[0] = stat_s[0]

    def query_part(c, carry):
        at = pl.ds(pl.multiple_of(c * width, width), width)
        hi, lo = eh[:, at], el[:, at]
        part_t = mm(ptr[:, :pass_dev], hi) + mm(ptr[:, :pass_dev], lo) + mm(ptr[:, pass_dev:], hi)
        u_s[pl.ds(c * GROUP, GROUP)] = part_t.T.reshape(GROUP, cap, emb)
        return carry

    lax.fori_loop(0, chunks, query_part, 0)
    u_r[0] = u_s[0]

    rest = stat_r.at[pl.ds(1, shards - 1)]
    to(rest, rest, stat_ss, stat_rs, peer(1)).wait_recv()
    top = jnp.concatenate([gather_row(stat_r, c, 0) for c in range(chunks)], axis=1)
    norm = jnp.concatenate([gather_row(stat_r, c, 1) for c in range(chunks)], axis=1)
    mask = disp[...] > 0.0
    peak = jnp.max(jnp.where(mask, top, LOW), axis=1, keepdims=True)
    gap = jnp.where(mask, top - peak, 0.0)
    mass = jnp.where(mask, norm * jnp.exp(gap), 0.0)
    total = jnp.sum(mass, axis=1, keepdims=True)
    share = mass / total
    log_target = logt[...]
    target = jnp.exp(log_target)
    coef = jnp.where(mask, (share - target) / norm, 0.0)
    coef_row = jnp.sum(coef, axis=0, keepdims=True)
    for c in range(chunks):
        coef_s[c] = coef_row[:, c * width : (c + 1) * width]

    def send_coef(j, carry):
        to(coef_s.at[j // GROUP], coef_r.at[j], coef_ss, coef_rs, peer(j)).start()
        return carry

    lax.fori_loop(1, shards, send_coef, 0)
    coef_r[0] = coef_s[0]

    def send_u(j, carry):
        to(u_s.at[j], u_r.at[j], u_ss, u_rs, source(j)).start()
        return carry

    lax.fori_loop(1, shards, send_u, 0)
    acoef[...] = coef * scale
    log_share = jnp.log(norm) + gap - jnp.log(total)
    term = jnp.where(mask, target * (log_target - log_share), 0.0)
    loss_ref[...] = jnp.sum(term, axis=1, keepdims=True)

    rest = coef_r.at[pl.ds(1, shards - 1)]
    to(rest, rest, coef_ss, coef_rs, peer(1)).wait_recv()
    for c in range(chunks):
        column = jnp.broadcast_to(gather_row(coef_r, c, 0), (width, width)).T
        rows = rows_r[c * GROUP : (c + 1) * GROUP].reshape(width, emb)
        hi, mid = split2(rows * column)
        rch[c * width : (c + 1) * width, :] = hi
        rcm[c * width : (c + 1) * width, :] = mid
    per = max(1, groups // 2)
    for h in range(0, groups, per):
        rows_at = slice(h * part, (h + per) * part)
        block = mm(eh[rows_at, :], rch[...]) + mm(el[rows_at, :], rch[...]) + mm(eh[rows_at, :], rcm[...])
        for i in range(h, h + per):
            d = order[i]
            z_s[d] = block[(i - h) * part : (i - h + 1) * part]
            if d != 0:
                to(
                    z_s.at[d], z_r.at[d], z_ss, z_rs, {"qb": lax.rem(qb + d, groups)}
                ).start()

    rest = u_r.at[pl.ds(1, shards - 1)]
    to(rest, rest, u_ss, u_rs, peer(1)).wait_recv()
    qg = jnp.zeros((per_dev, emb), F32)
    for c in range(chunks):
        ah, am = split2(acoef[:, c * width : (c + 1) * width])
        uh, um = split2(u_r[c * GROUP : (c + 1) * GROUP].reshape(width, emb))
        qg = qg + mm(ah, uh) + mm(am, uh) + mm(ah, um)
    qg_ref[...] = qg

    rest = z_r.at[pl.ds(1, groups - 1)]
    to(rest, rest, z_ss, z_rs, {"qb": lax.rem(qb + 1, groups)}).wait_recv()
    out = z_s[0]
    for d in range(1, groups):
        out = out + z_r[d]
    pg_ref[...] = out

    for ref, sem in (
        (meta_r, meta_ss),
        (rows_r, rows_ss),
        (stat_r, stat_ss),
        (coef_r, coef_ss),
        (u_r, u_ss),
    ):
        rest = ref.at[pl.ds(1, shards - 1)]
        to(rest, rest, sem, coef_rs, peer(1)).wait_send()
    rest = z_r.at[pl.ds(1, groups - 1)]
    to(rest, rest, z_ss, z_rs, {"qb": lax.rem(qb + 1, groups)}).wait_send()


def local(shards, groups, queries, reader_logits, probe_shards, probe_within, passages, list_sizes):
    per_dev, emb = queries.shape
    probes = probe_shards.shape[1]
    pass_dev = passages.shape[0]
    cap = min(per_dev, 16)
    chunks = shards // GROUP
    width = GROUP * cap
    slots = shards * cap
    part = pass_dev // groups
    vmem = pltpu.VMEM
    dma = pltpu.SemaphoreType.DMA
    any_spec = pl.BlockSpec(memory_space=pl.ANY)
    vmem_spec = pl.BlockSpec(memory_space=pltpu.VMEM)
    qg, pg, loss = pl.pallas_call(
        functools.partial(kernel, shards, groups, cap),
        out_shape=(
            jax.ShapeDtypeStruct((per_dev, emb), F32),
            jax.ShapeDtypeStruct((part, emb), F32),
            jax.ShapeDtypeStruct((per_dev, 1), F32),
        ),
        in_specs=[any_spec] * 6,
        out_specs=(vmem_spec,) * 3,
        scratch_shapes=[
            vmem((per_dev, emb), F32),
            vmem((per_dev, probes), F32),
            vmem((per_dev, probes), I32),
            vmem((per_dev, probes), I32),
            vmem((pass_dev, emb), F32),
            vmem(list_sizes.shape, I32),
            vmem((chunks, 1, width), F32),
            vmem((shards, 1, width), F32),
            vmem((shards, cap, emb), F32),
            vmem((shards, cap, emb), F32),
            vmem((chunks, 2, width), F32),
            vmem((shards, 2, width), F32),
            vmem((chunks, 1, width), F32),
            vmem((shards, 1, width), F32),
            vmem((shards, cap, emb), F32),
            vmem((shards, cap, emb), F32),
            vmem((groups, part, emb), F32),
            vmem((groups, part, emb), F32),
            vmem((shards, slots), BF16),
            vmem((per_dev, slots), F32),
            vmem((per_dev, slots), F32),
            vmem((per_dev, slots), F32),
            vmem((pass_dev, 6 * emb), BF16),
            vmem((emb, 2 * pass_dev), BF16),
            vmem((pass_dev, width), F32),
            vmem((pass_dev, slots), BF16),
            vmem((pass_dev, slots), BF16),
            vmem((slots, emb), BF16),
            vmem((slots, emb), BF16),
            dma((5 + groups,)),
            dma,
            dma((chunks,)),
            dma,
            dma((chunks,)),
            dma,
            dma,
            dma,
            dma,
            dma,
            dma,
            dma,
            dma,
        ],
        compiler_params=pltpu.CompilerParams(
            collective_id=0, has_side_effects=True, vmem_limit_bytes=40 * 1024 * 1024
        ),
    )(queries, reader_logits, probe_shards, probe_within, passages, list_sizes)
    return qg, pg, loss[:, 0]


def solution(mesh):
    return jax.shard_map(
        functools.partial(local, mesh.shape["lists"], mesh.shape["qb"]),
        mesh=mesh,
        in_specs=(
            P(("lists", "qb"), None),
            P(("lists", "qb"), None),
            P(("lists", "qb"), None),
            P(("lists", "qb"), None),
            P("lists", None),
            P("lists", None),
        ),
        out_specs=(P(("lists", "qb"), None), P(("lists", "qb"), None), P(("lists", "qb"))),
        check_vma=False,
    )
```

```python
import functools
import math

import jax
import jax.numpy as jnp
from jax import lax
from jax.experimental import pallas as pl
from jax.experimental.pallas import tpu as pltpu
from jax.sharding import PartitionSpec as P

MESH = pl.DeviceIdType.MESH
F32, BF16, I32 = jnp.float32, jnp.bfloat16, jnp.int32
LOW = -1e30
GROUP = 8


def split3(x):
    hi = x.astype(BF16)
    rest = x - hi.astype(F32)
    mid = rest.astype(BF16)
    low = (rest - mid.astype(F32)).astype(BF16)
    return hi, mid, low


def split2(x):
    hi = x.astype(BF16)
    return hi, (x - hi.astype(F32)).astype(BF16)


def mm(a, b):
    return jnp.dot(a, b, preferred_element_type=F32)


def mm_nt(a, b):
    return lax.dot_general(a, b, (((1,), (1,)), ((), ())), preferred_element_type=F32)


def mm_tn(a, b):
    return lax.dot_general(a, b, (((0,), (0,)), ((), ())), preferred_element_type=F32)


def kernel(
    shards,
    groups,
    cap,
    q_hbm,
    lg_hbm,
    ps_hbm,
    pw_hbm,
    p_hbm,
    ls_hbm,
    qg_ref,
    pg_ref,
    loss_ref,
    q_v,
    lg_v,
    ps_v,
    pw_v,
    p_v,
    ls_v,
    meta_s,
    meta_r,
    rows_s,
    rows_r,
    stat_s,
    stat_r,
    coef_s,
    coef_r,
    u_s,
    u_r,
    z_s,
    z_r,
    expand,
    disp,
    logt,
    acoef,
    pcat,
    ptr,
    owner,
    eh,
    el,
    rch,
    rcm,
    in_sem,
    meta_ss,
    meta_rs,
    rows_ss,
    rows_rs,
    stat_ss,
    stat_rs,
    coef_ss,
    coef_rs,
    u_ss,
    u_rs,
    z_ss,
    z_rs,
):
    per_dev, emb = q_v.shape
    probes = ps_v.shape[0]
    pass_dev = p_v.shape[0]
    part = pass_dev // groups
    chunks = shards // GROUP
    width = GROUP * cap
    slots = shards * cap
    scale = 1.0 / math.sqrt(emb)
    me = lax.axis_index("lists")
    qb = lax.axis_index("qb")

    def peer(j):
        return {"lists": lax.rem(me + j, shards)}

    def source(j):
        return {"lists": lax.rem(me - j + shards, shards)}

    def to(src, dst, ss, rs, device):
        return pltpu.make_async_remote_copy(
            src_ref=src, dst_ref=dst, send_sem=ss, recv_sem=rs, device_id=device, device_id_type=MESH
        )

    order = [3, 5, 4, 2, 6, 1, 7, 0]
    small = [(q_hbm, q_v), (ps_hbm, ps_v), (pw_hbm, pw_v), (lg_hbm, lg_v), (ls_hbm, ls_v)]
    loads = [pltpu.make_async_copy(a, b, in_sem.at[i]) for i, (a, b) in enumerate(small)]
    for i, d in enumerate(order):
        start = pl.multiple_of(lax.rem(qb + d, groups) * part, part)
        loads.append(
            pltpu.make_async_copy(
                p_hbm.at[pl.ds(start, part)], p_v.at[pl.ds(i * part, part)], in_sem.at[len(small) + i]
            )
        )
    for load in loads:
        load.start()

    barrier = pltpu.get_barrier_semaphore()

    def greet(j, carry):
        pl.semaphore_signal(barrier, inc=1, device_id=peer(j), device_id_type=MESH)
        return carry

    lax.fori_loop(1, shards, greet, 0)
    for d in range(1, groups):
        pl.semaphore_signal(
            barrier, inc=1, device_id={"qb": lax.rem(qb + d, groups)}, device_id_type=MESH
        )

    expand[...] = (
        lax.broadcasted_iota(I32, (shards, slots), 1) // cap
        == lax.broadcasted_iota(I32, (shards, slots), 0)
    ).astype(BF16)
    place = (lax.rem(lax.broadcasted_iota(I32, (per_dev, slots), 1), cap) + 1).astype(F32)
    tri = (
        lax.broadcasted_iota(I32, (per_dev, per_dev), 1)
        <= lax.broadcasted_iota(I32, (per_dev, per_dev), 0)
    ).astype(BF16)
    shard_lane = lax.broadcasted_iota(I32, (per_dev, shards), 1)
    for load in loads[:3]:
        load.wait()
    ps = ps_v[...]
    rel = jnp.where(ps >= me, ps - me, ps - me + shards).T
    within = pw_v[...].T + 1
    w1 = jnp.zeros((per_dev, shards), I32)
    for k in range(probes):
        w1 = jnp.where(rel[:, k : k + 1] == shard_lane, within[:, k : k + 1], w1)
    w1 = w1.astype(F32)
    hot = w1 > 0.0
    rank = mm(tri, hot.astype(BF16))
    slot1 = jnp.where(hot, rank, 0.0)
    both = mm(jnp.concatenate([slot1, w1], axis=0).astype(BF16), expand[...])
    mask = both[:per_dev] == place
    disp[...] = mask.astype(F32)
    ids = jnp.sum(jnp.where(mask, both[per_dev:], 0.0), axis=0, keepdims=True)
    for c in range(chunks):
        meta_s[c] = ids[:, c * width : (c + 1) * width]
    q_scaled = q_v[...] * scale
    q3 = jnp.concatenate(split3(q_scaled), axis=0)
    for c in range(chunks):
        d1 = disp[:, c * width : (c + 1) * width].astype(BF16)
        block = mm_tn(jnp.concatenate([d1, d1, d1], axis=0), q3)
        rows_s[pl.ds(c * GROUP, GROUP)] = block.reshape(GROUP, cap, emb)

    pl.semaphore_wait(barrier, shards - 1 + groups - 1)

    def send_meta(j, carry):
        c = j // GROUP
        to(meta_s.at[c], meta_r.at[j], meta_ss, meta_rs.at[c], peer(j)).start()
        return carry

    def send_rows(j, carry):
        c = j // GROUP
        to(rows_s.at[j], rows_r.at[j], rows_ss, rows_rs.at[c], peer(j)).start()
        return carry

    def send_both(j, carry):
        return send_rows(j, send_meta(j, carry))

    lax.fori_loop(1, shards, send_both, 0)
    meta_r[0] = meta_s[0]
    rows_r[0] = rows_s[0]

    for load in loads[3:]:
        load.wait()
    p = p_v[...]
    ph, pm, plow = split3(p)
    pcat[...] = jnp.concatenate([ph, pm, ph, plow, ph, pm], axis=1)
    pth, ptm = split2(p.T)
    ptr[:, :pass_dev] = pth
    ptr[:, pass_dev:] = ptm
    end = jnp.zeros((1, 1), I32)
    for i, d in enumerate(order):
        first = lax.rem(qb + d, groups) * part
        number = lax.broadcasted_iota(I32, (part, width), 0) + first
        end = jnp.zeros((1, 1), I32)
        own = jnp.ones((part, width), F32)
        for g in range(ls_v.shape[1]):
            end = end + ls_v[:, g : g + 1]
            own = own + jnp.where(number >= end, 1.0, 0.0)
        owner[i * part : (i + 1) * part, :] = own

    lg = lg_v[...]
    lg = lg - jnp.max(lg, axis=0, keepdims=True)
    lt = (lg - jnp.log(jnp.sum(jnp.exp(lg), axis=0, keepdims=True))).T
    lt_shard = jnp.zeros((per_dev, shards), F32)
    for k in range(probes):
        lt_shard = jnp.where(rel[:, k : k + 1] == shard_lane, lt[:, k : k + 1], lt_shard)
    lt3 = mm(jnp.concatenate(split3(lt_shard), axis=0), expand[...])
    logt[...] = lt3[:per_dev] + lt3[per_dev : 2 * per_dev] + lt3[2 * per_dev :]

    lane = lax.broadcasted_iota(I32, (1, width), 1) // cap

    def gather_row(ref, c, row):
        out = jnp.zeros((1, width), F32)
        for jj in range(GROUP):
            out = jnp.where(lane == jj, ref[c * GROUP + jj, row : row + 1, :], out)
        return out

    def wait_chunk(ref, sems, c):
        @pl.when(c == 0)
        def _():
            view = ref.at[pl.ds(1, GROUP - 1)]
            to(view, view, rows_ss, sems.at[0], peer(1)).wait_recv()

        @pl.when(c > 0)
        def _():
            view = ref.at[pl.ds(c * GROUP, GROUP)]
            to(view, view, rows_ss, sems.at[c], peer(1)).wait_recv()

    def forward(c, carry):
        wait_chunk(meta_r, meta_rs, c)
        ident = gather_row(meta_r, c, 0)
        wait_chunk(rows_r, rows_rs, c)
        rows = rows_r[pl.ds(c * GROUP, GROUP)].reshape(width, emb)
        rh, rm, rl = split3(rows)
        score = mm_nt(pcat[...], jnp.concatenate([rh, rh, rm, rh, rl, rm], axis=1))
        score = jnp.where(owner[...] == ident, score, LOW)
        top = jnp.max(score, axis=0, keepdims=True)
        expo = jnp.exp(score - top)
        norm = jnp.sum(expo, axis=0, keepdims=True)
        stat_s[c, 0:1, :] = top
        stat_s[c, 1:2, :] = norm

        def send_stat(jj, carry):
            j = c * GROUP + jj
            to(stat_s.at[c], stat_r.at[j], stat_ss, stat_rs, source(j)).start()
            return carry

        lax.fori_loop(jnp.where(c == 0, 1, 0), GROUP, send_stat, 0)
        hi, lo = split2(expo)
        at = pl.ds(pl.multiple_of(c * width, width), width)
        eh[:, at] = hi
        el[:, at] = lo
        return carry

    lax.fori_loop(0, chunks, forward, 0)
    stat_r[0] = stat_s[0]

    def query_part(c, carry):
        at = pl.ds(pl.multiple_of(c * width, width), width)
        hi, lo = eh[:, at], el[:, at]
        part_t = mm(ptr[:, :pass_dev], hi) + mm(ptr[:, :pass_dev], lo) + mm(ptr[:, pass_dev:], hi)
        u_s[pl.ds(c * GROUP, GROUP)] = part_t.T.reshape(GROUP, cap, emb)
        return carry

    lax.fori_loop(0, chunks, query_part, 0)
    u_r[0] = u_s[0]

    rest = stat_r.at[pl.ds(1, shards - 1)]
    to(rest, rest, stat_ss, stat_rs, peer(1)).wait_recv()
    top = jnp.concatenate([gather_row(stat_r, c, 0) for c in range(chunks)], axis=1)
    norm = jnp.concatenate([gather_row(stat_r, c, 1) for c in range(chunks)], axis=1)
    mask = disp[...] > 0.0
    peak = jnp.max(jnp.where(mask, top, LOW), axis=1, keepdims=True)
    gap = jnp.where(mask, top - peak, 0.0)
    mass = jnp.where(mask, norm * jnp.exp(gap), 0.0)
    total = jnp.sum(mass, axis=1, keepdims=True)
    share = mass / total
    log_target = logt[...]
    target = jnp.exp(log_target)
    coef = jnp.where(mask, (share - target) / norm, 0.0)
    coef_row = jnp.sum(coef, axis=0, keepdims=True)
    for c in range(chunks):
        coef_s[c] = coef_row[:, c * width : (c + 1) * width]

    def send_coef(j, carry):
        to(coef_s.at[j // GROUP], coef_r.at[j], coef_ss, coef_rs, peer(j)).start()
        return carry

    lax.fori_loop(1, shards, send_coef, 0)
    coef_r[0] = coef_s[0]

    def send_u(j, carry):
        to(u_s.at[j], u_r.at[j], u_ss, u_rs, source(j)).start()
        return carry

    lax.fori_loop(1, shards, send_u, 0)
    acoef[...] = coef * scale
    log_share = jnp.log(norm) + gap - jnp.log(total)
    term = jnp.where(mask, target * (log_target - log_share), 0.0)
    diagonal = lax.broadcasted_iota(I32, (per_dev, per_dev), 0) == lax.broadcasted_iota(
        I32, (per_dev, per_dev), 1
    )
    loss_ref[...] = jnp.sum(
        jnp.where(diagonal, jnp.sum(term, axis=1, keepdims=True), 0.0), axis=0, keepdims=True
    )

    rest = coef_r.at[pl.ds(1, shards - 1)]
    to(rest, rest, coef_ss, coef_rs, peer(1)).wait_recv()
    for c in range(chunks):
        column = jnp.broadcast_to(gather_row(coef_r, c, 0), (width, width)).T
        rows = rows_r[c * GROUP : (c + 1) * GROUP].reshape(width, emb)
        hi, mid = split2(rows * column)
        rch[c * width : (c + 1) * width, :] = hi
        rcm[c * width : (c + 1) * width, :] = mid
    rc = jnp.concatenate([rch[...], rcm[...]], axis=1)

    def passage_part(h):
        rows_at = slice(h * part, (h + groups // 2) * part)
        both = mm(eh[rows_at, :], rc) + mm(el[rows_at, :], rc)
        block = both[:, :emb] + both[:, emb:]
        for i in range(groups // 2):
            z_s[order[h + i]] = block[i * part : (i + 1) * part]

    half = part // 2
    first, second = pl.ds(0, half), pl.ds(half, half)

    def hop(src, slot, rows_at, step):
        device = {"qb": lax.rem(qb + step + groups, groups)}
        return to(src, z_r.at[slot].at[rows_at], z_ss.at[slot], z_rs.at[slot], device)

    every = pl.ds(0, part)
    passage_part(0)
    relays = [
        hop(z_s.at[3], 0, every, 1),
        hop(z_s.at[5], 1, every, -1),
        hop(z_s.at[4].at[first], 2, first, 2),
        hop(z_s.at[4].at[second], 3, second, -2),
    ]
    for copy in relays:
        copy.start()
    passage_part(groups // 2)
    direct = [hop(z_s.at[1], 4, every, 1), hop(z_s.at[7], 5, every, -1)]
    for copy in direct:
        copy.start()
    relays[0].wait_recv()
    relays[2].wait_recv()
    z_s[2] = z_s[2] + z_r[0]
    z_s[2, 0:half] = z_s[2, 0:half] + z_r[2, 0:half]
    direct.append(hop(z_s.at[2], 6, every, 2))
    direct[2].start()
    relays[1].wait_recv()
    relays[3].wait_recv()
    z_s[6] = z_s[6] + z_r[1]
    z_s[6, half:] = z_s[6, half:] + z_r[3, half:]
    direct.append(hop(z_s.at[6], 7, every, -2))
    direct[3].start()

    rest = u_r.at[pl.ds(1, shards - 1)]
    to(rest, rest, u_ss, u_rs, peer(1)).wait_recv()
    qg = jnp.zeros((per_dev, emb), F32)
    for c in range(chunks):
        ah, am = split2(acoef[:, c * width : (c + 1) * width])
        uh, um = split2(u_r[c * GROUP : (c + 1) * GROUP].reshape(width, emb))
        qg = qg + mm(ah, uh) + mm(am, uh) + mm(ah, um)
    qg_ref[...] = qg

    out = z_s[0]
    for slot, copy in enumerate(direct):
        copy.wait_recv()
        out = out + z_r[4 + slot]
    pg_ref[...] = out

    for ref, sem in (
        (meta_r, meta_ss),
        (rows_r, rows_ss),
        (stat_r, stat_ss),
        (coef_r, coef_ss),
        (u_r, u_ss),
    ):
        rest = ref.at[pl.ds(1, shards - 1)]
        to(rest, rest, sem, coef_rs, peer(1)).wait_send()
    for copy in relays + direct:
        copy.wait_send()


def store(qg_ref, pg_ref, loss_ref, qg_out, pg_out, loss_out, sems):
    pairs = ((pg_ref, pg_out), (qg_ref, qg_out), (loss_ref, loss_out))
    copies = [pltpu.make_async_copy(a, b, sems.at[i]) for i, (a, b) in enumerate(pairs)]
    for copy in copies:
        copy.start()
    for copy in copies:
        copy.wait()


def local(shards, groups, queries, reader_logits, probe_shards, probe_within, passages, list_sizes):
    per_dev, emb = queries.shape
    probes = probe_shards.shape[1]
    pass_dev = passages.shape[0]
    cap = min(per_dev, 16)
    chunks = shards // GROUP
    width = GROUP * cap
    slots = shards * cap
    part = pass_dev // groups
    vmem = pltpu.VMEM
    dma = pltpu.SemaphoreType.DMA
    hbm_spec = pl.BlockSpec(memory_space=pltpu.HBM)
    vmem_spec = pl.BlockSpec(memory_space=pltpu.VMEM)
    qg, pg, loss = pl.pallas_call(
        functools.partial(kernel, shards, groups, cap),
        out_shape=(
            jax.ShapeDtypeStruct((per_dev, emb), F32),
            jax.ShapeDtypeStruct((part, emb), F32),
            jax.ShapeDtypeStruct((1, per_dev), F32),
        ),
        in_specs=[hbm_spec] * 6,
        out_specs=(vmem_spec,) * 3,
        scratch_shapes=[
            vmem((per_dev, emb), F32),
            vmem((probes, per_dev), F32),
            vmem((probes, per_dev), I32),
            vmem((probes, per_dev), I32),
            vmem((pass_dev, emb), F32),
            vmem(list_sizes.shape, I32),
            vmem((chunks, 1, width), F32),
            vmem((shards, 1, width), F32),
            vmem((shards, cap, emb), F32),
            vmem((shards, cap, emb), F32),
            vmem((chunks, 2, width), F32),
            vmem((shards, 2, width), F32),
            vmem((chunks, 1, width), F32),
            vmem((shards, 1, width), F32),
            vmem((shards, cap, emb), F32),
            vmem((shards, cap, emb), F32),
            vmem((groups, part, emb), F32),
            vmem((groups, part, emb), F32),
            vmem((shards, slots), BF16),
            vmem((per_dev, slots), F32),
            vmem((per_dev, slots), F32),
            vmem((per_dev, slots), F32),
            vmem((pass_dev, 6 * emb), BF16),
            vmem((emb, 2 * pass_dev), BF16),
            vmem((pass_dev, width), F32),
            vmem((pass_dev, slots), BF16),
            vmem((pass_dev, slots), BF16),
            vmem((slots, emb), BF16),
            vmem((slots, emb), BF16),
            dma((5 + groups,)),
            dma,
            dma((chunks,)),
            dma,
            dma((chunks,)),
            dma,
            dma,
            dma,
            dma,
            dma,
            dma,
            dma((groups,)),
            dma((groups,)),
        ],
        compiler_params=pltpu.CompilerParams(
            collective_id=0, has_side_effects=True, vmem_limit_bytes=60 * 1024 * 1024
        ),
    )(queries, reader_logits.T, probe_shards.T, probe_within.T, passages, list_sizes)
    qg, pg, loss = pl.pallas_call(
        store,
        out_shape=tuple(jax.ShapeDtypeStruct(x.shape, F32) for x in (qg, pg, loss)),
        in_specs=[vmem_spec] * 3,
        out_specs=(hbm_spec,) * 3,
        scratch_shapes=[dma((3,))],
    )(qg, pg, loss)
    return qg, pg, loss.reshape(per_dev)


def solution(mesh):
    return jax.shard_map(
        functools.partial(local, mesh.shape["lists"], mesh.shape["qb"]),
        mesh=mesh,
        in_specs=(
            P(("lists", "qb"), None),
            P(("lists", "qb"), None),
            P(("lists", "qb"), None),
            P(("lists", "qb"), None),
            P("lists", None),
            P("lists", None),
        ),
        out_specs=(P(("lists", "qb"), None), P(("lists", "qb"), None), P(("lists", "qb"))),
        check_vma=False,
    )
```

```python
import functools
import math

import jax
import jax.numpy as jnp
from jax import lax
from jax.experimental import pallas as pl
from jax.experimental.pallas import tpu as pltpu
from jax.sharding import PartitionSpec as P

MESH = pl.DeviceIdType.MESH
F32, BF16, I32 = jnp.float32, jnp.bfloat16, jnp.int32
LOW = -1e30
GROUP = 8


def split3(x):
    hi = x.astype(BF16)
    rest = x - hi.astype(F32)
    mid = rest.astype(BF16)
    low = (rest - mid.astype(F32)).astype(BF16)
    return hi, mid, low


def split2(x):
    hi = x.astype(BF16)
    return hi, (x - hi.astype(F32)).astype(BF16)


def mm(a, b):
    return jnp.dot(a, b, preferred_element_type=F32)


def mm_nt(a, b):
    return lax.dot_general(a, b, (((1,), (1,)), ((), ())), preferred_element_type=F32)


def mm_tn(a, b):
    return lax.dot_general(a, b, (((0,), (0,)), ((), ())), preferred_element_type=F32)


def kernel(
    shards,
    groups,
    cap,
    q_hbm,
    lg_hbm,
    ps_hbm,
    pw_hbm,
    p_hbm,
    ls_hbm,
    qg_ref,
    pg_ref,
    loss_ref,
    q_v,
    lg_v,
    ps_v,
    pw_v,
    p_v,
    ls_v,
    blk,
    stat_s,
    stat_r,
    coef_s,
    coef_r,
    u_s,
    u_r,
    z_s,
    z_r,
    expand,
    disp,
    logt,
    acoef,
    pcat,
    ptr,
    owner,
    rank_of,
    same_of,
    want,
    wide,
    rows_s,
    rows_f,
    ident_s,
    ident,
    eh,
    el,
    rch,
    rcm,
    in_sem,
    y_ss,
    y_rs,
    rows_ss,
    rows_rs,
    ident_ss,
    ident_rs,
    stat_ss,
    stat_rs,
    coef_ss,
    coef_rs,
    u_ss,
    u_rs,
    z_ss,
    z_rs,
):
    per_dev, emb = q_v.shape
    probes = ps_v.shape[0]
    pass_dev = p_v.shape[0]
    part = pass_dev // groups
    chunks = shards // GROUP
    width = GROUP * cap
    slots = shards * cap
    lists_dev = ls_v.shape[1]
    scale = 1.0 / math.sqrt(emb)
    me = lax.axis_index("lists")
    qb = lax.axis_index("qb")

    nc, ny = 2, 8
    nx = shards // (nc * ny)
    x, y, core = me // (ny * nc), lax.rem(me // nc, ny), lax.rem(me, nc)

    def away(dx, dy, dc):
        there = lax.rem(x + dx, nx) * ny + lax.rem(y + dy, ny)
        return {"lists": there * nc + lax.rem(core + dc, nc)}

    def peer(c, dy):
        return away(c // nc, dy, c % nc)

    def source(c, dy):
        return away(nx - c // nc, ny - dy, c % nc)

    def to(src, dst, ss, rs, device):
        return pltpu.make_async_remote_copy(
            src_ref=src, dst_ref=dst, send_sem=ss, recv_sem=rs, device_id=device, device_id_type=MESH
        )

    order = [3, 5, 4, 2, 6, 1, 7, 0]
    small = [(q_hbm, q_v), (ps_hbm, ps_v), (pw_hbm, pw_v), (lg_hbm, lg_v), (ls_hbm, ls_v)]
    loads = [pltpu.make_async_copy(a, b, in_sem.at[i]) for i, (a, b) in enumerate(small)]
    for i, d in enumerate(order):
        start = pl.multiple_of(lax.rem(qb + d, groups) * part, part)
        loads.append(
            pltpu.make_async_copy(
                p_hbm.at[pl.ds(start, part)], p_v.at[pl.ds(i * part, part)], in_sem.at[len(small) + i]
            )
        )
    for load in loads:
        load.start()

    barrier = pltpu.get_barrier_semaphore()

    greeted = [away(0, dy, 0) for dy in (4, 3, 5, 2, 6, 1, 7)]
    greeted += [away(c // nc, 0, c % nc) for c in (4, 5, 2, 6, 3, 7, 1)]
    greeted += [{"qb": lax.rem(qb + d, groups)} for d in (2, groups - 2, 1, groups - 1)]
    for device in greeted:
        pl.semaphore_signal(barrier, inc=1, device_id=device, device_id_type=MESH)

    for load in loads[:3]:
        load.wait()
    ps = ps_v[...]
    code = (ps * lists_dev + pw_v[...]).astype(F32)
    blk[0, 0:per_dev, :] = q_v[...] * scale
    quarter = probes // 4
    blk[0, per_dev : per_dev + quarter, :] = jnp.concatenate(
        [code[i * quarter : (i + 1) * quarter] for i in range(4)], axis=1
    )
    used = pl.ds(0, per_dev + quarter)

    def block(j):
        return blk.at[j].at[used]

    def blocks(j, n):
        return blk.at[pl.ds(j, n), used]

    pl.semaphore_wait(barrier, len(greeted))
    for dy in (4, 3, 5, 2, 6, 1, 7):
        to(block(0), block(dy), y_ss, y_rs.at[dy], away(0, dy, 0)).start()

    for load in loads[3:]:
        load.wait()
    p = p_v[...]
    ph, pm, plow = split3(p)
    pcat[...] = jnp.concatenate([ph, pm, ph, plow, ph, pm], axis=1)
    pth, ptm = split2(p.T)
    ptr[:, :pass_dev] = pth
    ptr[:, pass_dev:] = ptm
    end = jnp.zeros((1, 1), I32)
    for i, d in enumerate(order):
        first = lax.rem(qb + d, groups) * part
        number = lax.broadcasted_iota(I32, (part, width), 0) + first
        end = jnp.zeros((1, 1), I32)
        own = jnp.ones((part, width), F32)
        for g in range(ls_v.shape[1]):
            end = end + ls_v[:, g : g + 1]
            own = own + jnp.where(number >= end, 1.0, 0.0)
        owner[i * part : (i + 1) * part, :] = own

    lane_q = lax.rem(lax.broadcasted_iota(I32, (4 * per_dev, GROUP * per_dev), 0), per_dev)
    wide_q = lax.rem(lax.broadcasted_iota(I32, (4 * per_dev, GROUP * per_dev), 1), per_dev)
    rank_of[...] = (lane_q <= wide_q).astype(BF16)
    same_of[...] = (lane_q == wide_q).astype(BF16)
    slot_at = lax.broadcasted_iota(I32, (width, GROUP * per_dev), 0)
    lane_at = lax.broadcasted_iota(I32, (width, GROUP * per_dev), 1)
    want[...] = jnp.where(
        lane_at // per_dev == slot_at // cap, lax.rem(slot_at, cap) + 1, -1
    ).astype(F32)

    diagonal = (
        lax.broadcasted_iota(I32, (GROUP, GROUP * per_dev), 1) // per_dev
        == lax.broadcasted_iota(I32, (GROUP, GROUP * per_dev), 0)
    )
    used_row = lax.broadcasted_iota(I32, (GROUP, 8, emb), 1) < quarter

    for dy in (1, 7, 2, 6, 3, 5, 4):
        to(block(dy), block(dy), y_ss, y_rs.at[dy], away(0, dy, 0)).wait_recv()
    wide[...] = jnp.concatenate(
        split3(blk[0:ny, 0:per_dev, :].reshape(ny * per_dev, emb)), axis=1
    )

    def compact(c, rows_out, ident_out):
        taker = away(c // nc, 0, c % nc)["lists"]
        number = blk[0:ny, per_dev : per_dev + 8, :] - (taker * lists_dev).astype(F32)
        found = used_row & (number >= 0.0) & (number < lists_dev)
        found = jnp.sum(jnp.where(found, number + 1.0, 0.0), axis=1)
        rank = mm((found > 0.0).astype(BF16), rank_of[...])
        one = mm(found.astype(BF16), same_of[...])
        slot = jnp.where(one > 0.0, rank, 0.0)
        slot = jnp.broadcast_to(slot[:, None, :], (GROUP, cap, GROUP * per_dev))
        pick = (slot.reshape(width, GROUP * per_dev) == want[...]).astype(BF16)
        picked = mm(pick, wide[...])
        hi, mid, low = (picked[:, i * emb : (i + 1) * emb] for i in range(3))
        rows_out[c] = (hi + mid) + low
        number = mm_nt(jnp.where(diagonal, one, 0.0).astype(BF16), pick)
        ident_out[c] = jnp.sum(number, axis=0, keepdims=True)

    def handed(c):
        taker = away(c // nc, 0, c % nc)
        return (
            to(rows_s.at[c], rows_f.at[c], rows_ss, rows_rs.at[c], taker),
            to(ident_s.at[c], ident.at[c], ident_ss, ident_rs.at[c], taker),
        )

    for c in (2, 6, 3, 7, 4, 5, 1):
        compact(c, rows_s, ident_s)
        for copy in handed(c):
            copy.start()
    compact(0, rows_f, ident)

    expand[...] = (
        lax.broadcasted_iota(I32, (shards, slots), 1) // cap
        == lax.broadcasted_iota(I32, (shards, slots), 0)
    ).astype(BF16)
    place = (lax.rem(lax.broadcasted_iota(I32, (per_dev, slots), 1), cap) + 1).astype(F32)
    tri = (
        lax.broadcasted_iota(I32, (per_dev, per_dev), 1)
        <= lax.broadcasted_iota(I32, (per_dev, per_dev), 0)
    ).astype(BF16)
    shard_lane = lax.broadcasted_iota(I32, (per_dev, shards), 1)
    dx = lax.rem(ps // (ny * nc) - x + nx, nx)
    dy = lax.rem(lax.rem(ps // nc, ny) - y + ny, ny)
    dc = lax.rem(lax.rem(ps, nc) - core + nc, nc)
    rel = ((dx * nc + dc) * ny + dy).T
    lg = lg_v[...]
    lg = lg - jnp.max(lg, axis=0, keepdims=True)
    lt = (lg - jnp.log(jnp.sum(jnp.exp(lg), axis=0, keepdims=True))).T
    hot = jnp.zeros((per_dev, shards), F32)
    lt_shard = jnp.zeros((per_dev, shards), F32)
    for k in range(probes):
        here = rel[:, k : k + 1] == shard_lane
        hot = jnp.where(here, 1.0, hot)
        lt_shard = jnp.where(here, lt[:, k : k + 1], lt_shard)
    slot1 = jnp.where(hot > 0.0, mm(tri, hot.astype(BF16)), 0.0)
    spread = mm(slot1.astype(BF16), expand[...])
    disp[...] = (spread == place).astype(F32)
    lt3 = mm(jnp.concatenate(split3(lt_shard), axis=0), expand[...])
    logt[...] = lt3[:per_dev] + lt3[per_dev : 2 * per_dev] + lt3[2 * per_dev :]

    lane = lax.broadcasted_iota(I32, (1, width), 1) // cap

    def gather_row(ref, c, row):
        out = jnp.zeros((1, width), F32)
        for jj in range(GROUP):
            out = jnp.where(lane == jj, ref[c * GROUP + jj, row : row + 1, :], out)
        return out

    def forward(dx, carry):
        at = pl.ds(pl.multiple_of(dx * nc * width, nc * width), nc * width)

        @pl.when(dx > 0)
        def _():
            for copy in handed(nc * dx):
                copy.wait_recv()

        for copy in handed(nc * dx + 1):
            copy.wait_recv()
        hi, mid, low = split3(rows_f[pl.ds(nc * dx, nc)].reshape(nc * width, emb))
        score = mm_nt(pcat[...], jnp.concatenate([hi, hi, mid, hi, low, mid], axis=1))
        number = jnp.concatenate([ident[nc * dx], ident[nc * dx + 1]], axis=1)
        held = jnp.concatenate([owner[...]] * nc, axis=1)
        score = jnp.where(held == number, score, LOW)
        top = jnp.max(score, axis=0, keepdims=True)
        expo = jnp.exp(score - top)
        norm = jnp.sum(expo, axis=0, keepdims=True)
        for k in range(nc):
            c = nc * dx + k
            stat_s[c, 0:1, :] = top[:, k * width : (k + 1) * width]
            stat_s[c, 1:2, :] = norm[:, k * width : (k + 1) * width]
        for k in range(nc):
            c = nc * dx + k
            send_chunk(c, lambda j: stat_s.at[c], stat_r, stat_ss, stat_rs, source)
        hi, lo = split2(expo)
        eh[:, at] = hi
        el[:, at] = lo
        return carry

    def send_chunk(c, src, dst, ss, rs, device):
        for dy in (4, 3, 5, 2, 6, 1, 7, 0):
            j = c * ny + dy
            if dy:
                to(src(j), dst.at[j], ss, rs, device(c, dy)).start()
            else:

                @pl.when(c > 0)
                def _():
                    to(src(j), dst.at[j], ss, rs, device(c, 0)).start()

    def send_all(src, dst, ss, rs, device):
        def one(i, carry):
            c = lax.rem(i + chunks // 2, chunks)
            send_chunk(c, lambda j: src(c, j), dst, ss, rs, device)
            return carry

        lax.fori_loop(0, chunks, one, 0)

    def in_turn(i, carry):
        return forward(jnp.where(i < 2, i, 5 - i), carry)

    lax.fori_loop(0, nx, in_turn, 0)
    stat_r[0] = stat_s[0]

    def query_part(i, carry):
        at = pl.ds(pl.multiple_of(i * nc * width, nc * width), nc * width)
        hi, lo = eh[:, at], el[:, at]
        part_t = mm(ptr[:, :pass_dev], hi) + mm(ptr[:, :pass_dev], lo) + mm(ptr[:, pass_dev:], hi)
        u_s[pl.ds(i * nc * GROUP, nc * GROUP)] = part_t.T.reshape(nc * GROUP, cap, emb)
        return carry

    lax.fori_loop(0, nx, query_part, 0)
    u_r[0] = u_s[0]

    rest = stat_r.at[pl.ds(1, shards - 1)]
    to(rest, rest, stat_ss, stat_rs, away(0, 0, 1)).wait_recv()
    top = jnp.concatenate([gather_row(stat_r, c, 0) for c in range(chunks)], axis=1)
    norm = jnp.concatenate([gather_row(stat_r, c, 1) for c in range(chunks)], axis=1)
    mask = disp[...] > 0.0
    peak = jnp.max(jnp.where(mask, top, LOW), axis=1, keepdims=True)
    gap = jnp.where(mask, top - peak, 0.0)
    mass = jnp.where(mask, norm * jnp.exp(gap), 0.0)
    total = jnp.sum(mass, axis=1, keepdims=True)
    share = mass / total
    log_target = logt[...]
    target = jnp.exp(log_target)
    coef = jnp.where(mask, (share - target) / norm, 0.0)
    coef_row = jnp.sum(coef, axis=0, keepdims=True)
    for c in range(chunks):
        coef_s[c] = coef_row[:, c * width : (c + 1) * width]

    send_all(lambda c, j: coef_s.at[c], coef_r, coef_ss, coef_rs, peer)
    coef_r[0] = coef_s[0]
    send_all(lambda c, j: u_s.at[j], u_r, u_ss, u_rs, source)
    acoef[...] = coef * scale
    log_share = jnp.log(norm) + gap - jnp.log(total)
    term = jnp.where(mask, target * (log_target - log_share), 0.0)
    diagonal = lax.broadcasted_iota(I32, (per_dev, per_dev), 0) == lax.broadcasted_iota(
        I32, (per_dev, per_dev), 1
    )
    loss_ref[...] = jnp.sum(
        jnp.where(diagonal, jnp.sum(term, axis=1, keepdims=True), 0.0), axis=0, keepdims=True
    )

    rest = coef_r.at[pl.ds(1, shards - 1)]
    to(rest, rest, coef_ss, coef_rs, away(0, 0, 1)).wait_recv()
    for c in range(chunks):
        column = jnp.broadcast_to(gather_row(coef_r, c, 0), (width, width)).T
        hi, mid = split2(rows_f[c] * column)
        rch[c * width : (c + 1) * width, :] = hi
        rcm[c * width : (c + 1) * width, :] = mid
    rc = jnp.concatenate([rch[...], rcm[...]], axis=1)

    def passage_part(h):
        rows_at = slice(h * part, (h + groups // 2) * part)
        both = mm(eh[rows_at, :], rc) + mm(el[rows_at, :], rc)
        block = both[:, :emb] + both[:, emb:]
        for i in range(groups // 2):
            z_s[order[h + i]] = block[i * part : (i + 1) * part]

    half = part // 2
    first, second = pl.ds(0, half), pl.ds(half, half)

    def hop(src, slot, rows_at, step):
        device = {"qb": lax.rem(qb + step + groups, groups)}
        return to(src, z_r.at[slot].at[rows_at], z_ss.at[slot], z_rs.at[slot], device)

    every = pl.ds(0, part)
    passage_part(0)
    relays = [
        hop(z_s.at[3], 0, every, 1),
        hop(z_s.at[5], 1, every, -1),
        hop(z_s.at[4].at[first], 2, first, 2),
        hop(z_s.at[4].at[second], 3, second, -2),
    ]
    for copy in relays:
        copy.start()
    passage_part(groups // 2)
    direct = [hop(z_s.at[1], 4, every, 1), hop(z_s.at[7], 5, every, -1)]
    for copy in direct:
        copy.start()
    relays[0].wait_recv()
    relays[2].wait_recv()
    z_s[2] = z_s[2] + z_r[0]
    z_s[2, 0:half] = z_s[2, 0:half] + z_r[2, 0:half]
    direct.append(hop(z_s.at[2], 6, every, 2))
    direct[2].start()
    relays[1].wait_recv()
    relays[3].wait_recv()
    z_s[6] = z_s[6] + z_r[1]
    z_s[6, half:] = z_s[6, half:] + z_r[3, half:]
    direct.append(hop(z_s.at[6], 7, every, -2))
    direct[3].start()

    rest = u_r.at[pl.ds(1, shards - 1)]
    to(rest, rest, u_ss, u_rs, away(0, 0, 1)).wait_recv()
    qg = jnp.zeros((per_dev, emb), F32)
    for c in range(chunks):
        ah, am = split2(acoef[:, c * width : (c + 1) * width])
        uh, um = split2(u_r[c * GROUP : (c + 1) * GROUP].reshape(width, emb))
        qg = qg + mm(ah, uh) + mm(am, uh) + mm(ah, um)
    qg_ref[...] = qg

    out = z_s[0]
    for slot, copy in enumerate(direct):
        copy.wait_recv()
        out = out + z_r[4 + slot]
    pg_ref[...] = out

    for view, sem in (
        (blocks(1, ny - 1), y_ss),
        (rows_f.at[pl.ds(1, chunks - 1)], rows_ss),
        (ident.at[pl.ds(1, chunks - 1)], ident_ss),
        (stat_r.at[pl.ds(1, shards - 1)], stat_ss),
        (coef_r.at[pl.ds(1, shards - 1)], coef_ss),
        (u_r.at[pl.ds(1, shards - 1)], u_ss),
    ):
        to(view, view, sem, coef_rs, away(0, 0, 1)).wait_send()
    for copy in relays + direct:
        copy.wait_send()


def store(qg_ref, pg_ref, loss_ref, qg_out, pg_out, loss_out, sems):
    pairs = ((pg_ref, pg_out), (qg_ref, qg_out), (loss_ref, loss_out))
    copies = [pltpu.make_async_copy(a, b, sems.at[i]) for i, (a, b) in enumerate(pairs)]
    for copy in copies:
        copy.start()
    for copy in copies:
        copy.wait()


def local(shards, groups, queries, reader_logits, probe_shards, probe_within, passages, list_sizes):
    per_dev, emb = queries.shape
    probes = probe_shards.shape[1]
    pass_dev = passages.shape[0]
    cap = min(per_dev, 16)
    chunks = shards // GROUP
    width = GROUP * cap
    slots = shards * cap
    part = pass_dev // groups
    vmem = pltpu.VMEM
    dma = pltpu.SemaphoreType.DMA
    hbm_spec = pl.BlockSpec(memory_space=pltpu.HBM)
    vmem_spec = pl.BlockSpec(memory_space=pltpu.VMEM)
    qg, pg, loss = pl.pallas_call(
        functools.partial(kernel, shards, groups, cap),
        out_shape=(
            jax.ShapeDtypeStruct((per_dev, emb), F32),
            jax.ShapeDtypeStruct((part, emb), F32),
            jax.ShapeDtypeStruct((1, per_dev), F32),
        ),
        in_specs=[hbm_spec] * 6,
        out_specs=(vmem_spec,) * 3,
        scratch_shapes=[
            vmem((per_dev, emb), F32),
            vmem((probes, per_dev), F32),
            vmem((probes, per_dev), I32),
            vmem((probes, per_dev), I32),
            vmem((pass_dev, emb), F32),
            vmem(list_sizes.shape, I32),
            vmem((8, per_dev + 8, emb), F32),
            vmem((chunks, 2, width), F32),
            vmem((shards, 2, width), F32),
            vmem((chunks, 1, width), F32),
            vmem((shards, 1, width), F32),
            vmem((shards, cap, emb), F32),
            vmem((shards, cap, emb), F32),
            vmem((groups, part, emb), F32),
            vmem((groups, part, emb), F32),
            vmem((shards, slots), BF16),
            vmem((per_dev, slots), F32),
            vmem((per_dev, slots), F32),
            vmem((per_dev, slots), F32),
            vmem((pass_dev, 6 * emb), BF16),
            vmem((emb, 2 * pass_dev), BF16),
            vmem((pass_dev, width), F32),
            vmem((4 * per_dev, GROUP * per_dev), BF16),
            vmem((4 * per_dev, GROUP * per_dev), BF16),
            vmem((width, GROUP * per_dev), F32),
            vmem((GROUP * per_dev, 3 * emb), BF16),
            vmem((chunks, width, emb), F32),
            vmem((chunks, width, emb), F32),
            vmem((chunks, 1, width), F32),
            vmem((chunks, 1, width), F32),
            vmem((pass_dev, slots), BF16),
            vmem((pass_dev, slots), BF16),
            vmem((slots, emb), BF16),
            vmem((slots, emb), BF16),
            dma((5 + groups,)),
            dma,
            dma((8,)),
            dma,
            dma((8,)),
            dma,
            dma((8,)),
            dma,
            dma,
            dma,
            dma,
            dma,
            dma,
            dma((groups,)),
            dma((groups,)),
        ],
        compiler_params=pltpu.CompilerParams(
            collective_id=0, has_side_effects=True, vmem_limit_bytes=60 * 1024 * 1024
        ),
    )(queries, reader_logits.T, probe_shards.T, probe_within.T, passages, list_sizes)
    qg, pg, loss = pl.pallas_call(
        store,
        out_shape=tuple(jax.ShapeDtypeStruct(x.shape, F32) for x in (qg, pg, loss)),
        in_specs=[vmem_spec] * 3,
        out_specs=(hbm_spec,) * 3,
        scratch_shapes=[dma((3,))],
    )(qg, pg, loss)
    return qg, pg, loss.reshape(per_dev)


def solution(mesh):
    return jax.shard_map(
        functools.partial(local, mesh.shape["lists"], mesh.shape["qb"]),
        mesh=mesh,
        in_specs=(
            P(("lists", "qb"), None),
            P(("lists", "qb"), None),
            P(("lists", "qb"), None),
            P(("lists", "qb"), None),
            P("lists", None),
            P("lists", None),
        ),
        out_specs=(P(("lists", "qb"), None), P(("lists", "qb"), None), P(("lists", "qb"))),
        check_vma=False,
    )
```

```python
import functools
import math

import jax
import jax.numpy as jnp
from jax import lax
from jax.experimental import pallas as pl
from jax.experimental.pallas import tpu as pltpu
from jax.sharding import PartitionSpec as P

MESH = pl.DeviceIdType.MESH
F32, BF16, I32 = jnp.float32, jnp.bfloat16, jnp.int32
LOW = -1e30
GROUP = 8


def split3(x):
    hi = x.astype(BF16)
    rest = x - hi.astype(F32)
    mid = rest.astype(BF16)
    low = (rest - mid.astype(F32)).astype(BF16)
    return hi, mid, low


def split2(x):
    hi = x.astype(BF16)
    return hi, (x - hi.astype(F32)).astype(BF16)


def mm(a, b):
    return jnp.dot(a, b, preferred_element_type=F32)


def mm_nt(a, b):
    return lax.dot_general(a, b, (((1,), (1,)), ((), ())), preferred_element_type=F32)


def mm_tn(a, b):
    return lax.dot_general(a, b, (((0,), (0,)), ((), ())), preferred_element_type=F32)


def kernel(
    shards,
    groups,
    cap,
    q_hbm,
    lg_hbm,
    ps_hbm,
    pw_hbm,
    p_hbm,
    ls_hbm,
    qg_hbm,
    pg_hbm,
    loss_hbm,
    qg_ref,
    pg_ref,
    loss_ref,
    q_v,
    lg_v,
    ps_v,
    pw_v,
    p_v,
    ls_v,
    blk,
    stat_s,
    stat_r,
    coef_s,
    coef_r,
    u_s,
    u_r,
    z_s,
    z_r,
    expand,
    disp,
    logt,
    acoef,
    pcat,
    ptr,
    owner,
    rank_of,
    same_of,
    want,
    wide,
    rows_s,
    rows_f,
    ident_s,
    ident,
    eh,
    el,
    rch,
    rcm,
    in_sem,
    out_sem,
    y_ss,
    y_rs,
    rows_ss,
    rows_rs,
    ident_ss,
    ident_rs,
    stat_ss,
    stat_rs,
    coef_ss,
    coef_rs,
    u_ss,
    u_rs,
    z_ss,
    z_rs,
):
    per_dev, emb = q_v.shape
    probes = ps_v.shape[0]
    pass_dev = p_v.shape[0]
    part = pass_dev // groups
    chunks = shards // GROUP
    width = GROUP * cap
    slots = shards * cap
    lists_dev = ls_v.shape[1]
    scale = 1.0 / math.sqrt(emb)
    me = lax.axis_index("lists")
    qb = lax.axis_index("qb")

    nc, ny = 2, 8
    nx = shards // (nc * ny)
    x, y, core = me // (ny * nc), lax.rem(me // nc, ny), lax.rem(me, nc)

    def away(dx, dy, dc):
        there = lax.rem(x + dx, nx) * ny + lax.rem(y + dy, ny)
        return {"lists": there * nc + lax.rem(core + dc, nc)}

    def peer(c, dy):
        return away(c // nc, dy, c % nc)

    def source(c, dy):
        return away(nx - c // nc, ny - dy, c % nc)

    def to(src, dst, ss, rs, device):
        return pltpu.make_async_remote_copy(
            src_ref=src, dst_ref=dst, send_sem=ss, recv_sem=rs, device_id=device, device_id_type=MESH
        )

    barrier = pltpu.get_barrier_semaphore()

    greeted = [{"qb": lax.rem(qb + d, groups)} for d in (2, groups - 2, 1, groups - 1)]
    greeted += [away(0, dy, 0) for dy in (4, 3, 5, 2, 6, 1, 7)]
    greeted += [away(c // nc, 0, c % nc) for c in (4, 5, 2, 6, 3, 7, 1)]
    for device in greeted:
        pl.semaphore_signal(barrier, inc=1, device_id=device, device_id_type=MESH)

    order = [4, 3, 5, 2, 6, 1, 7, 0]
    small = [(q_hbm, q_v), (ps_hbm, ps_v), (pw_hbm, pw_v), (lg_hbm, lg_v), (ls_hbm, ls_v)]
    loads = [pltpu.make_async_copy(a, b, in_sem.at[i]) for i, (a, b) in enumerate(small)]
    for i, d in enumerate(order):
        start = pl.multiple_of(lax.rem(qb + d, groups) * part, part)
        loads.append(
            pltpu.make_async_copy(
                p_hbm.at[pl.ds(start, part)], p_v.at[pl.ds(i * part, part)], in_sem.at[len(small) + i]
            )
        )
    for load in loads:
        load.start()

    for load in loads[:3]:
        load.wait()
    ps = ps_v[...]
    code = (ps * lists_dev + pw_v[...]).astype(F32)
    blk[0, 0:per_dev, :] = q_v[...] * scale
    quarter = probes // 4
    blk[0, per_dev : per_dev + quarter, :] = jnp.concatenate(
        [code[i * quarter : (i + 1) * quarter] for i in range(4)], axis=1
    )
    used = pl.ds(0, per_dev + quarter)

    def block(j):
        return blk.at[j].at[used]

    def blocks(j, n):
        return blk.at[pl.ds(j, n), used]

    pl.semaphore_wait(barrier, len(greeted))
    for dy in (4, 3, 5, 2, 6, 1, 7):
        to(block(0), block(dy), y_ss, y_rs.at[dy], away(0, dy, 0)).start()

    for load in loads[3:]:
        load.wait()
    p = p_v[...]
    ph, pm, plow = split3(p)
    pcat[...] = jnp.concatenate([ph, pm, ph, plow, ph, pm], axis=1)
    pth, ptm = split2(p.T)
    ptr[:, :pass_dev] = pth
    ptr[:, pass_dev:] = ptm
    end = jnp.zeros((1, 1), I32)
    for i, d in enumerate(order):
        first = lax.rem(qb + d, groups) * part
        number = lax.broadcasted_iota(I32, (part, width), 0) + first
        end = jnp.zeros((1, 1), I32)
        own = jnp.ones((part, width), F32)
        for g in range(ls_v.shape[1]):
            end = end + ls_v[:, g : g + 1]
            own = own + jnp.where(number >= end, 1.0, 0.0)
        owner[i * part : (i + 1) * part, :] = own

    lane_q = lax.rem(lax.broadcasted_iota(I32, (4 * per_dev, GROUP * per_dev), 0), per_dev)
    wide_q = lax.rem(lax.broadcasted_iota(I32, (4 * per_dev, GROUP * per_dev), 1), per_dev)
    rank_of[...] = (lane_q <= wide_q).astype(BF16)
    same_of[...] = (lane_q == wide_q).astype(BF16)
    slot_at = lax.broadcasted_iota(I32, (width, GROUP * per_dev), 0)
    lane_at = lax.broadcasted_iota(I32, (width, GROUP * per_dev), 1)
    want[...] = jnp.where(
        lane_at // per_dev == slot_at // cap, lax.rem(slot_at, cap) + 1, -1
    ).astype(F32)

    diagonal = (
        lax.broadcasted_iota(I32, (GROUP, GROUP * per_dev), 1) // per_dev
        == lax.broadcasted_iota(I32, (GROUP, GROUP * per_dev), 0)
    )
    used_row = lax.broadcasted_iota(I32, (GROUP, 8, emb), 1) < quarter

    for dy in (1, 7, 2, 6, 3, 5, 4):
        to(block(dy), block(dy), y_ss, y_rs.at[dy], away(0, dy, 0)).wait_recv()
    wide[...] = jnp.concatenate(
        split3(blk[0:ny, 0:per_dev, :].reshape(ny * per_dev, emb)), axis=1
    )

    codes = blk[0:ny, per_dev : per_dev + 8, :]
    found = []
    for c in range(chunks):
        taker = away(c // nc, 0, c % nc)["lists"]
        number = codes - (taker * lists_dev).astype(F32)
        here = used_row & (number >= 0.0) & (number < lists_dev)
        found.append(jnp.sum(jnp.where(here, number + 1.0, 0.0), axis=1))
    found = jnp.concatenate(found, axis=0)
    rank = mm((found > 0.0).astype(BF16), rank_of[...])
    one = mm(found.astype(BF16), same_of[...])
    slot = jnp.where(one > 0.0, rank, 0.0)

    def compact(c, rows_out, ident_out):
        mine = slice(c * GROUP, (c + 1) * GROUP)
        wanted = jnp.broadcast_to(slot[mine][:, None, :], (GROUP, cap, GROUP * per_dev))
        pick = (wanted.reshape(width, GROUP * per_dev) == want[...]).astype(BF16)
        picked = mm(pick, wide[...])
        hi, mid, low = (picked[:, i * emb : (i + 1) * emb] for i in range(3))
        rows_out[c] = (hi + mid) + low
        number = mm_nt(jnp.where(diagonal, one[mine], 0.0).astype(BF16), pick)
        ident_out[c] = jnp.sum(number, axis=0, keepdims=True)

    def handed(c):
        taker = away(c // nc, 0, c % nc)
        return (
            to(rows_s.at[c], rows_f.at[c], rows_ss, rows_rs.at[c], taker),
            to(ident_s.at[c], ident.at[c], ident_ss, ident_rs.at[c], taker),
        )

    for pair in ((2, 6), (3, 7), (4, 5), (1,)):
        for c in pair:
            compact(c, rows_s, ident_s)
        for c in pair:
            for copy in handed(c):
                copy.start()
    compact(0, rows_f, ident)

    expand[...] = (
        lax.broadcasted_iota(I32, (shards, slots), 1) // cap
        == lax.broadcasted_iota(I32, (shards, slots), 0)
    ).astype(BF16)
    place = (lax.rem(lax.broadcasted_iota(I32, (per_dev, slots), 1), cap) + 1).astype(F32)
    tri = (
        lax.broadcasted_iota(I32, (per_dev, per_dev), 1)
        <= lax.broadcasted_iota(I32, (per_dev, per_dev), 0)
    ).astype(BF16)
    shard_lane = lax.broadcasted_iota(I32, (per_dev, shards), 1)
    dx = lax.rem(ps // (ny * nc) - x + nx, nx)
    dy = lax.rem(lax.rem(ps // nc, ny) - y + ny, ny)
    dc = lax.rem(lax.rem(ps, nc) - core + nc, nc)
    rel = ((dx * nc + dc) * ny + dy).T
    lg = lg_v[...]
    lg = lg - jnp.max(lg, axis=0, keepdims=True)
    lt = (lg - jnp.log(jnp.sum(jnp.exp(lg), axis=0, keepdims=True))).T
    hot = jnp.zeros((per_dev, shards), F32)
    lt_shard = jnp.zeros((per_dev, shards), F32)
    for k in range(probes):
        here = rel[:, k : k + 1] == shard_lane
        hot = jnp.where(here, 1.0, hot)
        lt_shard = jnp.where(here, lt[:, k : k + 1], lt_shard)
    slot1 = jnp.where(hot > 0.0, mm(tri, hot.astype(BF16)), 0.0)
    spread = mm(slot1.astype(BF16), expand[...])
    disp[...] = (spread == place).astype(F32)
    lt3 = mm(jnp.concatenate(split3(lt_shard), axis=0), expand[...])
    logt[...] = lt3[:per_dev] + lt3[per_dev : 2 * per_dev] + lt3[2 * per_dev :]

    lane = lax.broadcasted_iota(I32, (1, width), 1) // cap

    def gather_row(ref, c, row):
        out = jnp.zeros((1, width), F32)
        for jj in range(GROUP):
            out = jnp.where(lane == jj, ref[c * GROUP + jj, row : row + 1, :], out)
        return out

    def forward(dx, carry):
        at = pl.ds(pl.multiple_of(dx * nc * width, nc * width), nc * width)

        @pl.when(dx > 0)
        def _():
            for copy in handed(nc * dx):
                copy.wait_recv()

        for copy in handed(nc * dx + 1):
            copy.wait_recv()
        hi, mid, low = split3(rows_f[pl.ds(nc * dx, nc)].reshape(nc * width, emb))
        score = mm_nt(pcat[...], jnp.concatenate([hi, hi, mid, hi, low, mid], axis=1))
        number = jnp.concatenate([ident[nc * dx], ident[nc * dx + 1]], axis=1)
        held = jnp.concatenate([owner[...]] * nc, axis=1)
        score = jnp.where(held == number, score, LOW)
        top = jnp.max(score, axis=0, keepdims=True)
        expo = jnp.exp(score - top)
        norm = jnp.sum(expo, axis=0, keepdims=True)
        for k in range(nc):
            c = nc * dx + k
            stat_s[c, 0:1, :] = top[:, k * width : (k + 1) * width]
            stat_s[c, 1:2, :] = norm[:, k * width : (k + 1) * width]
        for k in range(nc):
            c = nc * dx + k
            send_chunk(c, lambda j: stat_s.at[c], stat_r, stat_ss, stat_rs, source)
        hi, lo = split2(expo)
        eh[:, at] = hi
        el[:, at] = lo
        return carry

    def send_chunk(c, src, dst, ss, rs, device):
        for dy in (4, 3, 5, 2, 6, 1, 7, 0):
            j = c * ny + dy
            if dy:
                to(src(j), dst.at[j], ss, rs, device(c, dy)).start()
            else:

                @pl.when(c > 0)
                def _():
                    to(src(j), dst.at[j], ss, rs, device(c, 0)).start()

    def send_all(src, dst, ss, rs, device):
        def one(i, carry):
            c = lax.rem(i + chunks // 2, chunks)
            send_chunk(c, lambda j: src(c, j), dst, ss, rs, device)
            return carry

        lax.fori_loop(0, chunks, one, 0)

    def in_turn(i, carry):
        return forward(jnp.where(i < 2, i, 5 - i), carry)

    lax.fori_loop(0, nx, in_turn, 0)
    stat_r[0] = stat_s[0]

    def query_part(i, carry):
        at = pl.ds(pl.multiple_of(i * nc * width, nc * width), nc * width)
        hi, lo = eh[:, at], el[:, at]
        part_t = mm(ptr[:, :pass_dev], hi) + mm(ptr[:, :pass_dev], lo) + mm(ptr[:, pass_dev:], hi)
        u_s[pl.ds(i * nc * GROUP, nc * GROUP)] = part_t.T.reshape(nc * GROUP, cap, emb)
        return carry

    lax.fori_loop(0, nx, query_part, 0)
    u_r[0] = u_s[0]

    rest = stat_r.at[pl.ds(1, shards - 1)]
    to(rest, rest, stat_ss, stat_rs, away(0, 0, 1)).wait_recv()
    top = jnp.concatenate([gather_row(stat_r, c, 0) for c in range(chunks)], axis=1)
    norm = jnp.concatenate([gather_row(stat_r, c, 1) for c in range(chunks)], axis=1)
    mask = disp[...] > 0.0
    peak = jnp.max(jnp.where(mask, top, LOW), axis=1, keepdims=True)
    gap = jnp.where(mask, top - peak, 0.0)
    mass = jnp.where(mask, norm * jnp.exp(gap), 0.0)
    total = jnp.sum(mass, axis=1, keepdims=True)
    share = mass / total
    log_target = logt[...]
    target = jnp.exp(log_target)
    coef = jnp.where(mask, (share - target) / norm, 0.0)
    coef_row = jnp.sum(coef, axis=0, keepdims=True)
    for c in range(chunks):
        coef_s[c] = coef_row[:, c * width : (c + 1) * width]

    send_all(lambda c, j: coef_s.at[c], coef_r, coef_ss, coef_rs, peer)
    coef_r[0] = coef_s[0]
    send_all(lambda c, j: u_s.at[j], u_r, u_ss, u_rs, source)
    acoef[...] = coef * scale
    log_share = jnp.log(norm) + gap - jnp.log(total)
    term = jnp.where(mask, target * (log_target - log_share), 0.0)
    diagonal = lax.broadcasted_iota(I32, (per_dev, per_dev), 0) == lax.broadcasted_iota(
        I32, (per_dev, per_dev), 1
    )
    loss_ref[...] = jnp.sum(
        jnp.where(diagonal, jnp.sum(term, axis=1, keepdims=True), 0.0), axis=0, keepdims=True
    )
    stores = [pltpu.make_async_copy(loss_ref, loss_hbm, out_sem.at[0])]
    stores[0].start()

    rest = coef_r.at[pl.ds(1, shards - 1)]
    to(rest, rest, coef_ss, coef_rs, away(0, 0, 1)).wait_recv()
    for c in range(chunks):
        column = jnp.broadcast_to(gather_row(coef_r, c, 0), (width, width)).T
        hi, mid = split2(rows_f[c] * column)
        rch[c * width : (c + 1) * width, :] = hi
        rcm[c * width : (c + 1) * width, :] = mid
    rc = jnp.concatenate([rch[...], rcm[...]], axis=1)

    def passage_part(h, n):
        rows_at = slice(h * part, (h + n) * part)
        both = mm(eh[rows_at, :], rc) + mm(el[rows_at, :], rc)
        block = both[:, :emb] + both[:, emb:]
        for i in range(n):
            z_s[order[h + i]] = block[i * part : (i + 1) * part]

    half = part // 2
    first, second = pl.ds(0, half), pl.ds(half, half)

    def hop(src, slot, rows_at, step):
        device = {"qb": lax.rem(qb + step + groups, groups)}
        return to(src, z_r.at[slot].at[rows_at], z_ss.at[slot], z_rs.at[slot], device)

    every = pl.ds(0, part)
    relays = [
        hop(z_s.at[3], 0, every, 1),
        hop(z_s.at[5], 1, every, -1),
        hop(z_s.at[4].at[first], 2, first, 2),
        hop(z_s.at[4].at[second], 3, second, -2),
    ]
    passage_part(0, 2)
    for i in (2, 3, 0):
        relays[i].start()
    passage_part(2, 2)
    relays[1].start()
    passage_part(4, 4)
    direct = [hop(z_s.at[1], 4, every, 1), hop(z_s.at[7], 5, every, -1)]
    for copy in direct:
        copy.start()
    relays[0].wait_recv()
    relays[2].wait_recv()
    z_s[2] = z_s[2] + z_r[0]
    z_s[2, 0:half] = z_s[2, 0:half] + z_r[2, 0:half]
    direct.append(hop(z_s.at[2], 6, every, 2))
    direct[2].start()
    relays[1].wait_recv()
    relays[3].wait_recv()
    z_s[6] = z_s[6] + z_r[1]
    z_s[6, half:] = z_s[6, half:] + z_r[3, half:]
    direct.append(hop(z_s.at[6], 7, every, -2))
    direct[3].start()

    rest = u_r.at[pl.ds(1, shards - 1)]
    to(rest, rest, u_ss, u_rs, away(0, 0, 1)).wait_recv()
    qg = jnp.zeros((per_dev, emb), F32)
    for c in range(chunks):
        ah, am = split2(acoef[:, c * width : (c + 1) * width])
        uh, um = split2(u_r[c * GROUP : (c + 1) * GROUP].reshape(width, emb))
        qg = qg + mm(ah, uh) + mm(am, uh) + mm(ah, um)
    qg_ref[...] = qg
    stores.append(pltpu.make_async_copy(qg_ref, qg_hbm, out_sem.at[1]))
    stores[1].start()

    out = z_s[0]
    for slot, copy in enumerate(direct):
        copy.wait_recv()
        out = out + z_r[4 + slot]
    pg_ref[...] = out
    stores.append(pltpu.make_async_copy(pg_ref, pg_hbm, out_sem.at[2]))
    stores[2].start()

    for view, sem in (
        (blocks(1, ny - 1), y_ss),
        (rows_f.at[pl.ds(1, chunks - 1)], rows_ss),
        (ident.at[pl.ds(1, chunks - 1)], ident_ss),
        (stat_r.at[pl.ds(1, shards - 1)], stat_ss),
        (coef_r.at[pl.ds(1, shards - 1)], coef_ss),
        (u_r.at[pl.ds(1, shards - 1)], u_ss),
    ):
        to(view, view, sem, coef_rs, away(0, 0, 1)).wait_send()
    for copy in relays + direct:
        copy.wait_send()
    for copy in stores:
        copy.wait()


def store(qg_ref, pg_ref, loss_ref, qg_out, pg_out, loss_out, sems):
    pairs = ((pg_ref, pg_out), (qg_ref, qg_out), (loss_ref, loss_out))
    copies = [pltpu.make_async_copy(a, b, sems.at[i]) for i, (a, b) in enumerate(pairs)]
    for copy in copies:
        copy.start()
    for copy in copies:
        copy.wait()


def local(shards, groups, queries, reader_logits, probe_shards, probe_within, passages, list_sizes):
    per_dev, emb = queries.shape
    probes = probe_shards.shape[1]
    pass_dev = passages.shape[0]
    cap = min(per_dev, 16)
    chunks = shards // GROUP
    width = GROUP * cap
    slots = shards * cap
    part = pass_dev // groups
    vmem = pltpu.VMEM
    dma = pltpu.SemaphoreType.DMA
    hbm_spec = pl.BlockSpec(memory_space=pltpu.HBM)
    vmem_spec = pl.BlockSpec(memory_space=pltpu.VMEM)
    qg, pg, loss = pl.pallas_call(
        functools.partial(kernel, shards, groups, cap),
        out_shape=(
            jax.ShapeDtypeStruct((per_dev, emb), F32),
            jax.ShapeDtypeStruct((part, emb), F32),
            jax.ShapeDtypeStruct((1, per_dev), F32),
        ),
        in_specs=[hbm_spec] * 6,
        out_specs=(hbm_spec,) * 3,
        scratch_shapes=[
            vmem((per_dev, emb), F32),
            vmem((part, emb), F32),
            vmem((1, per_dev), F32),
            vmem((per_dev, emb), F32),
            vmem((probes, per_dev), F32),
            vmem((probes, per_dev), I32),
            vmem((probes, per_dev), I32),
            vmem((pass_dev, emb), F32),
            vmem(list_sizes.shape, I32),
            vmem((8, per_dev + 8, emb), F32),
            vmem((chunks, 2, width), F32),
            vmem((shards, 2, width), F32),
            vmem((chunks, 1, width), F32),
            vmem((shards, 1, width), F32),
            vmem((shards, cap, emb), F32),
            vmem((shards, cap, emb), F32),
            vmem((groups, part, emb), F32),
            vmem((groups, part, emb), F32),
            vmem((shards, slots), BF16),
            vmem((per_dev, slots), F32),
            vmem((per_dev, slots), F32),
            vmem((per_dev, slots), F32),
            vmem((pass_dev, 6 * emb), BF16),
            vmem((emb, 2 * pass_dev), BF16),
            vmem((pass_dev, width), F32),
            vmem((4 * per_dev, GROUP * per_dev), BF16),
            vmem((4 * per_dev, GROUP * per_dev), BF16),
            vmem((width, GROUP * per_dev), F32),
            vmem((GROUP * per_dev, 3 * emb), BF16),
            vmem((chunks, width, emb), F32),
            vmem((chunks, width, emb), F32),
            vmem((chunks, 1, width), F32),
            vmem((chunks, 1, width), F32),
            vmem((pass_dev, slots), BF16),
            vmem((pass_dev, slots), BF16),
            vmem((slots, emb), BF16),
            vmem((slots, emb), BF16),
            dma((5 + groups,)),
            dma((3,)),
            dma,
            dma((8,)),
            dma,
            dma((8,)),
            dma,
            dma((8,)),
            dma,
            dma,
            dma,
            dma,
            dma,
            dma,
            dma((groups,)),
            dma((groups,)),
        ],
        compiler_params=pltpu.CompilerParams(
            collective_id=0, has_side_effects=True, vmem_limit_bytes=60 * 1024 * 1024
        ),
    )(queries, reader_logits.T, probe_shards.T, probe_within.T, passages, list_sizes)
    qg, pg, loss = pl.pallas_call(
        store,
        out_shape=tuple(jax.ShapeDtypeStruct(x.shape, F32) for x in (qg, pg, loss)),
        in_specs=[vmem_spec] * 3,
        out_specs=(hbm_spec,) * 3,
        scratch_shapes=[dma((3,))],
    )(qg, pg, loss)
    return qg, pg, loss.reshape(per_dev)


def solution(mesh):
    return jax.shard_map(
        functools.partial(local, mesh.shape["lists"], mesh.shape["qb"]),
        mesh=mesh,
        in_specs=(
            P(("lists", "qb"), None),
            P(("lists", "qb"), None),
            P(("lists", "qb"), None),
            P(("lists", "qb"), None),
            P("lists", None),
            P("lists", None),
        ),
        out_specs=(P(("lists", "qb"), None), P(("lists", "qb"), None), P(("lists", "qb"))),
        check_vma=False,
    )
```
